512 devices in a mesh: layer: 2 (over z_hi), row: 16 (over z_lo, x), col: 16 (over y, core).
Axes of the slice: x: 4, y: 8, z: 8 (z_hi: 2, z_lo: 4; z = z_hi * 4 + z_lo), core: 2. Of those that a mesh axis runs over, the one named last changes fastest.
Arguments:
- trail: bfloat16 [16384, 2, 16384], P('row', 'layer', 'col'), may hold values from -6 to 6
- lower_panels: bfloat16 [2, 2, 256, 16384], P('layer', None, 'col', 'row'), may hold values from -6 to 6
- upper_panels: bfloat16 [2, 2, 256, 2, 16384], P('layer', None, 'row', None, 'col'), may hold values from -0.375 to 0.375
- lower_inverse: bfloat16 [2, 2, 256, 256], P('layer'), may hold values from -0.375 to 0.375
- upper_inverse: bfloat16 [2, 2, 256, 256], P('layer'), may hold values from -0.375 to 0.375
- above_block: bfloat16 [2, 256, 256], P('layer'), may hold values from -0.375 to 0.375
- left_block: bfloat16 [2, 256, 256], P('layer'), may hold values from -0.375 to 0.375
- row_order: int32 [2, 2, 256], P('layer'), may hold values from 0 to 255, each once within a row
- row_mask: int32 [2, 2, 64], P('layer', None, 'row'), may hold values 0 or 1
- column_mask: int32 [2, 2, 2, 64], P('layer', None, None, 'col'), may hold values 0 or 1
Outputs:
- updated: bfloat16 [16384, 2, 16384], P('row', 'layer', 'col')
The draws below stay inside these ranges and needn't reach their ends.
Inputs may be any that keep to these rules, and one draw needn't show every extreme that they name: Each row_order[l,k] is a permutation of 0 to 255.
All inputs are finite; a program needn't handle non-finite values. No bound on the sum of `row_mask` or of `column_mask` on one device may be relied on, other than what follows from the above.
Results may differ from the reference program's by a relative error of at most 0.012.
Values may be sent and summed in bfloat16 or wider, within the bound.
A program may use at most 64 MiB of HBM per device.

```python
import jax
import jax.numpy as jnp
from jax import lax

NB = 256
CBH = 4
R = 64
CH = 16384
N_COL = 16


def touch_ends(array, rng, low, high):
    place = [jax.random.randint(jax.random.fold_in(rng, axis), (), 0, length) for axis, length in enumerate(array.shape)]
    widest = array.shape.index(max(array.shape))
    next_to = place[:widest] + [(place[widest] + 1) % array.shape[widest]] + place[widest + 1:]
    return array.at[tuple(place)].set(low).at[tuple(next_to)].set(high)


def block_scale(own_key, shape, split, smallest, top_value):
    gain = 1.0
    for dim, parts in split:
        draws = jax.random.uniform(jax.random.fold_in(jax.random.fold_in(own_key, 6), dim), (parts,), jnp.float32, smallest / len(split), top_value / len(split))
        gain = gain * jnp.repeat(jnp.exp(draws), shape[dim] // parts).reshape((-1,) + (1,) * (len(shape) - 1 - dim))
    return gain


def gaussian(key, shape, spread, most, shards=(), kind=jnp.bfloat16):
    values = jax.random.normal(key, shape, jnp.float32) * spread
    if len(shards) > 0:
        values = block_scale(key, shape, shards, -0.22, 0.18) * values
    return jnp.clip(values, min=-most, max=most).astype(kind)


def setup_inputs(seed: int = 0) -> dict:
    key_list = jax.random.split(jax.random.key(seed), 11)
    trail = gaussian(key_list[0], (R * NB, 2, CH), 1.0, 6.0, ((0, 16), (1, 2), (2, 16)))
    lower_panels = gaussian(key_list[1], (2, 2, NB, R * NB), 1.0, 6.0, ((0, 2), (2, 16), (3, 16)))
    upper_panels = gaussian(key_list[2], (2, 2, NB, 2, CH), 0.0625, 0.375, ((0, 2), (2, 16), (4, 16)))
    lower_inverse = gaussian(key_list[3], (2, 2, NB, NB), NB ** -0.5, 0.375, ((0, 2),))
    upper_inverse = gaussian(key_list[4], (2, 2, NB, NB), NB ** -0.5, 0.375, ((0, 2),))
    above_block = gaussian(key_list[5], (2, NB, NB), 0.0625, 0.375, ((0, 2),))
    left_block = gaussian(key_list[6], (2, NB, NB), 0.0625, 0.375, ((0, 2),))
    row_order = jax.vmap(lambda own: jax.random.permutation(own, NB))(jax.random.split(key_list[7], 2 * 2)).reshape((2, 2, NB)).astype(jnp.int32)
    row_mask = touch_ends((jax.random.randint(key_list[8], (2, 2, R), 0, 4) < 3).astype(jnp.int32), jax.random.fold_in(key_list[8], 1), 0, 1)
    column_mask = touch_ends((jax.random.randint(key_list[9], (2, 2, 2, CBH * N_COL), 0, 4) < 3).astype(jnp.int32), jax.random.fold_in(key_list[9], 1), 0, 1)
    return {"trail": trail, "lower_panels": lower_panels, "upper_panels": upper_panels, "lower_inverse": lower_inverse, "upper_inverse": upper_inverse, "above_block": above_block, "left_block": left_block, "row_order": row_order, "row_mask": row_mask, "column_mask": column_mask}


def build_factors(cols_all, rows_flat, low_inv, up_inv, above, left, order, lmask, umask):
    nb = cols_all.shape[1]
    rows_scale = jnp.repeat(lmask.astype(jnp.float32), nb, axis=1)
    cols_scale = jnp.repeat(umask.astype(jnp.float32), nb, axis=2).reshape(2, -1)
    upper_first = (jnp.dot(low_inv[0], jnp.take(rows_flat[0], order[0], axis=0), preferred_element_type=jnp.float32) * cols_scale[0]).astype(jnp.bfloat16)
    lower_first = (lax.dot_general(cols_all[0], up_inv[0], (((0,), (0,)), ((), ())), preferred_element_type=jnp.float32) * rows_scale[0][:, None]).astype(jnp.bfloat16)
    upper_cross = jnp.dot(low_inv[0], jnp.take(above, order[0], axis=0), preferred_element_type=jnp.float32).astype(jnp.bfloat16)
    lower_cross = jnp.dot(left, up_inv[0], preferred_element_type=jnp.float32).astype(jnp.bfloat16)
    column_next = (cols_all[1].T.astype(jnp.float32) - jnp.dot(lower_first, upper_cross, preferred_element_type=jnp.float32)).astype(jnp.bfloat16)
    row_next = (rows_flat[1].astype(jnp.float32) - jnp.dot(lower_cross, upper_first, preferred_element_type=jnp.float32)).astype(jnp.bfloat16)
    upper_second = (jnp.dot(low_inv[1], jnp.take(row_next, order[1], axis=0), preferred_element_type=jnp.float32) * cols_scale[1]).astype(jnp.bfloat16)
    lower_second = (jnp.dot(column_next, up_inv[1], preferred_element_type=jnp.float32) * rows_scale[1][:, None]).astype(jnp.bfloat16)
    return lower_first, upper_first, lower_second, upper_second


def reference(trail, lower_panels, upper_panels, lower_inverse, upper_inverse, above_block, left_block, row_order, row_mask, column_mask):
    lowers = []
    uppers = []
    for layer_idx in range(2):
        rows_flat = upper_panels[layer_idx].reshape(2, NB, 2 * CH)
        lower_first, upper_first, lower_second, upper_second = build_factors(
            lower_panels[layer_idx], rows_flat, lower_inverse[layer_idx], upper_inverse[layer_idx],
            above_block[layer_idx], left_block[layer_idx], row_order[layer_idx], row_mask[layer_idx], column_mask[layer_idx])
        lowers.append(jnp.stack([lower_first, lower_second]))
        uppers.append(jnp.stack([upper_first, upper_second]))
    low_all = jnp.stack(lowers).reshape(2, 2, R, NB, NB)
    low_all = jnp.moveaxis(low_all, 2, 0)
    up_all = jnp.stack(uppers)
    trail_blocks = trail.reshape(R, NB, 2 * CH)

    def one_block(pair):
        block_low, block_trail = pair
        total = block_trail.astype(jnp.float32)
        for layer_idx in range(2):
            part = -(jnp.dot(block_low[layer_idx, 0], up_all[layer_idx, 0], preferred_element_type=jnp.float32)
                     + jnp.dot(block_low[layer_idx, 1], up_all[layer_idx, 1], preferred_element_type=jnp.float32))
            part = lax.optimization_barrier(part.astype(jnp.bfloat16)).astype(jnp.float32)
            total = total + part
        return total.astype(jnp.bfloat16)

    result = lax.map(one_block, (low_all, trail_blocks))
    return result.reshape(R * NB, 2, CH)
```

```python
import functools

import jax
import jax.numpy as jnp
from jax import lax
from jax.experimental import pallas as pl
from jax.experimental.pallas import tpu as pltpu
from jax.sharding import PartitionSpec as P

NZ, NX, NY = 4, 4, 8
NB = 256
SUB = 16
W = 1024
PANEL = 2 * W
CROSS = PANEL + 6 * NB
M0, M1, V, UI0, UI1, WW = (PANEL + i * NB for i in range(6))
F32, BF16 = jnp.float32, jnp.bfloat16


def dot(a, b):
    return jnp.dot(a, b, preferred_element_type=F32)


def dot_tn(a, b):
    return lax.dot_general(a, b, (((0,), (0,)), ((), ())), preferred_element_type=F32)


def dot_nt(a, b):
    return lax.dot_general(a, b, (((1,), (1,)), ((), ())), preferred_element_type=F32)


def kernel(
    trail_ref, lp_ref, uh_ref, li_ref, ui_ref, above_ref, left_ref, order_ref, rmask_ref, cmask_ref,
    out_ref,
    lo, xb, stage, uo, uc, own, masks, xmasks, lf, uf, acc, trail_v, out_v,
    send, recv, local,
):
    layer = lax.axis_index("layer")
    row = lax.axis_index("row")
    col = lax.axis_index("col")
    zl, x, y, core = row // NX, row % NX, col // 2, col % 2

    def at(dl=0, dz=0, dx=0, dy=0, dc=0):
        return (
            (layer + dl) % 2,
            (zl + dz + NZ) % NZ * NX + (x + dx + NX) % NX,
            (y + dy + NY) % NY * 2 + (core + dc) % 2,
        )

    def lslot(dy, dc=0):
        return pl.ds(pl.multiple_of(((y + dy + NY) % NY * 2 + (core + dc) % 2) * SUB, SUB), SUB)

    def uslot(dz, dx):
        return pl.ds(
            pl.multiple_of(((zl + dz + NZ) % NZ * NX + (x + dx + NX) % NX) * SUB, SUB), SUB
        )

    barrier = pltpu.get_barrier_semaphore()
    peers = [dict(dy=1), dict(dy=-1), dict(dx=1), dict(dx=-1), dict(dz=1), dict(dz=2), dict(dz=3),
             dict(dl=1), dict(dc=1)]
    for p in peers:
        pl.semaphore_signal(barrier, 1, device_id=at(**p), device_id_type=pl.DeviceIdType.MESH)

    fetch = pltpu.make_async_copy(trail_ref, trail_v, local.at[0])
    fetch.start()

    for k in range(2):
        stage[:, pl.ds(k * W, W)] = lp_ref[k]
    lo[lslot(0)] = stage[:, :PANEL]
    uo[uslot(0, 0)] = uh_ref[layer]
    masks[...] = jnp.zeros_like(masks)
    masks[0:2, 0:4] = rmask_ref[...].astype(F32)
    for k in range(2):
        for h in range(2):
            r = 2 + 2 * h + k
            masks[r : r + 1, 0:4] = cmask_ref[k, h : h + 1, :].astype(F32)

    place = lax.broadcasted_iota(jnp.int32, (NB, NB), 0)

    def permuted(rows, k):
        hot = jnp.where(place == order_ref[k : k + 1, :], 1.0, 0.0).astype(BF16)
        return dot_nt(rows, hot).astype(BF16)

    share = lslot(0)
    m0 = permuted(li_ref[0, share], 0)
    m1 = permuted(li_ref[1, share], 1)
    lower_cross = dot(left_ref[...], ui_ref[0]).astype(BF16)
    upper_cross = dot(m0, above_ref[...]).astype(BF16)
    for place_at, value in (
        (M0, m0),
        (M1, m1),
        (V, dot(m1, lower_cross).astype(BF16)),
        (UI0, ui_ref[0, share]),
        (UI1, ui_ref[1, share]),
        (WW, dot(upper_cross, ui_ref[1]).astype(BF16)),
    ):
        stage[:, pl.ds(place_at, NB)] = value

    pl.semaphore_wait(barrier, len(peers))

    used = [0]
    started = []

    def new(src, dst, to):
        i = used[0]
        used[0] += 1
        return pltpu.make_async_remote_copy(
            src_ref=src, dst_ref=dst, send_sem=send.at[i], recv_sem=recv.at[i],
            device_id=at(**to), device_id_type=pl.DeviceIdType.MESH,
        )

    def go(ref, to, dst=None):
        copy = new(ref, ref if dst is None else dst, to)
        copy.start()
        started.append(copy)
        return copy

    cx = go(stage, dict(dl=1), xb.at[share])
    cu = go(uh_ref.at[1 - layer], dict(dl=1), uc.at[uslot(0, 0)])
    cm = go(masks, dict(dl=1), xmasks)

    class Ring:
        def __init__(self, buf, width):
            self.buf, self.width, self.half = buf, width, width // 2
            self.sib = []

        def slot(self, dy, part=None):
            if part is None:
                return self.buf.at[lslot(dy)]
            return self.buf.at[lslot(dy), pl.ds(part * self.half, self.half)]

        def begin(self):
            self.up = go(self.slot(0), dict(dy=1))
            self.down = go(self.slot(0), dict(dy=-1))
            self.sib.append(go(self.slot(0), dict(dc=1)))

        def step(self, s):
            self.up.wait_recv()
            if s < 3:
                nup = go(self.slot(-s), dict(dy=1))
            elif s == 3:
                nup = go(self.slot(-3, 0), dict(dy=1))
            self.down.wait_recv()
            if s < 3:
                ndown = go(self.slot(s), dict(dy=-1))
            elif s == 3:
                ndown = go(self.slot(3, 1), dict(dy=-1))
            if s < 4:
                self.sib.append(go(self.slot(-s), dict(dc=1)))
                self.sib.append(go(self.slot(s), dict(dc=1)))
                self.up, self.down = nup, ndown
            else:
                self.sib.append(go(self.slot(4), dict(dc=1)))

        def end(self):
            for c in self.sib:
                c.wait_recv()

    class Plane:
        def __init__(self, buf):
            self.buf = buf
            self.z, self.p, self.m, self.f, self.g = {}, {}, {}, {}, {}

        def slot(self, dz, dx, part=None):
            if part is None:
                return self.buf.at[uslot(dz, dx)]
            return self.buf.at[uslot(dz, dx), pl.ds(part * W, W)]

        def begin(self):
            self.p[0] = go(self.slot(0, 0), dict(dx=1))
            self.m[0] = go(self.slot(0, 0), dict(dx=-1))
            for d in (1, 3, 2):
                self.z[d] = go(self.slot(0, 0), dict(dz=d))

        def spread(self, d):
            self.z[d].wait_recv()
            self.p[d] = go(self.slot(-d, 0), dict(dx=1))
            self.m[d] = go(self.slot(-d, 0), dict(dx=-1))

        def forward(self, d):
            self.p[d].wait_recv()
            self.f[d] = go(self.slot(-d, -1, 0), dict(dx=1))
            self.m[d].wait_recv()
            self.g[d] = go(self.slot(-d, 1, 1), dict(dx=-1))

        def end(self):
            for d in range(4):
                self.f[d].wait_recv()
                self.g[d].wait_recv()

    ring0, ring1 = Ring(lo, PANEL), Ring(xb, CROSS)
    plane0, plane1 = Plane(uo), Plane(uc)

    def lower_factors(i, buf, ui0, ui1, w, mask):
        for b in range(4):
            rows = pl.ds(b * NB, NB)
            first = (dot_tn(buf[:, pl.ds(b * NB, NB)], ui0) * mask[0:1, b : b + 1]).astype(BF16)
            second = dot_tn(buf[:, pl.ds(W + b * NB, NB)], ui1) - dot(first, w)
            lf[i, rows, 0:NB] = first
            lf[i, rows, NB : 2 * NB] = (second * mask[1:2, b : b + 1]).astype(BF16)

    def upper_factors(i, buf, m0, m1, v, mask):
        c0 = mask[pl.ds(2 + 2 * layer, 1), :]
        c1 = mask[pl.ds(3 + 2 * layer, 1), :]
        for b in range(4):
            cols = pl.ds(b * NB, NB)
            first = (dot(m0, buf[:, cols]) * c0[:, b : b + 1]).astype(BF16)
            second = dot(m1, buf[:, pl.ds(W + b * NB, NB)]) - dot(v, first)
            uf[i, 0:NB, cols] = first
            uf[i, NB : 2 * NB, cols] = (second * c1[:, b : b + 1]).astype(BF16)

    def product(i, b):
        return dot(lf[i, pl.ds(b * NB, NB)], uf[i])

    ring0.begin()
    plane0.begin()
    own[0] = permuted(li_ref[0], 0)
    own[1] = permuted(li_ref[1], 1)
    own[2] = dot(own[1], lower_cross).astype(BF16)
    own[3] = dot(dot(own[0], above_ref[...]).astype(BF16), ui_ref[1]).astype(BF16)

    ring0.step(1)
    plane0.forward(0)
    plane0.spread(1)
    plane0.spread(3)
    plane0.spread(2)
    ring0.step(2)
    cu.wait_recv()
    plane1.begin()
    cx.wait_recv()
    ring1.begin()
    ring0.step(3)
    plane0.forward(1)
    plane0.forward(3)
    ring1.step(1)
    plane1.forward(0)
    plane0.forward(2)
    ring0.step(4)
    ring0.end()
    ring1.step(2)
    plane1.spread(1)
    plane1.spread(3)
    plane1.spread(2)
    lower_factors(0, lo, ui_ref[0], ui_ref[1], own[3], masks)
    ring1.step(3)
    plane1.forward(1)
    plane1.forward(3)
    plane1.forward(2)
    plane0.end()
    upper_factors(0, uo, own[0], own[1], own[2], masks)
    ring1.step(4)

    @pl.loop(0, 4)
    def _(b):
        acc[pl.ds(pl.multiple_of(b * NB, NB), NB)] = product(0, b)

    ring1.end()
    cm.wait_recv()
    lower_factors(
        1, xb, xb[:, pl.ds(UI0, NB)], xb[:, pl.ds(UI1, NB)], xb[:, pl.ds(WW, NB)], xmasks
    )
    plane1.end()
    upper_factors(1, uc, xb[:, pl.ds(M0, NB)], xb[:, pl.ds(M1, NB)], xb[:, pl.ds(V, NB)], xmasks)
    fetch.wait()

    @pl.loop(0, 4)
    def _(b):
        rows = pl.ds(pl.multiple_of(b * NB, NB), NB)
        total = acc[rows] + product(1, b)
        out_v[rows] = (trail_v[rows].astype(F32) - total).astype(BF16)

    put = pltpu.make_async_copy(out_v, out_ref, local.at[1])
    put.start()
    for c in started:
        c.wait_send()
    put.wait()


def on_device(trail, lower, upper, li, ui, above, left, order, rmask, cmask):
    halves = jnp.transpose(upper[0], (2, 1, 0, 3)).reshape(2, SUB, PANEL)
    vmem = pl.BlockSpec(memory_space=pltpu.VMEM)
    hbm = pl.BlockSpec(memory_space=pl.ANY)
    n = 96
    out = pl.pallas_call(
        kernel,
        out_shape=jax.ShapeDtypeStruct((W, W), BF16),
        in_specs=[hbm] + [vmem] * 9,
        out_specs=hbm,
        scratch_shapes=[
            pltpu.VMEM((NB, PANEL), BF16),
            pltpu.VMEM((NB, CROSS), BF16),
            pltpu.VMEM((SUB, CROSS), BF16),
            pltpu.VMEM((NB, PANEL), BF16),
            pltpu.VMEM((NB, PANEL), BF16),
            pltpu.VMEM((4, NB, NB), BF16),
            pltpu.VMEM((8, 128), F32),
            pltpu.VMEM((8, 128), F32),
            pltpu.VMEM((2, W, 2 * NB), BF16),
            pltpu.VMEM((2, 2 * NB, W), BF16),
            pltpu.VMEM((W, W), F32),
            pltpu.VMEM((W, W), BF16),
            pltpu.VMEM((W, W), BF16),
            pltpu.SemaphoreType.DMA((n,)),
            pltpu.SemaphoreType.DMA((n,)),
            pltpu.SemaphoreType.DMA((2,)),
        ],
        compiler_params=pltpu.CompilerParams(
            collective_id=0, has_side_effects=True, vmem_limit_bytes=48 * 2**20
        ),
        name="panels_update",
    )(trail[:, 0, :], lower[0], halves, li[0], ui[0], above[0], left[0], order[0], rmask[0], cmask[0])
    return out[:, None, :]


def solution(mesh):
    placed = (
        P("row", "layer", "col"),
        P("layer", None, "col", "row"),
        P("layer", None, "row", None, "col"),
        P("layer", None, None, None),
        P("layer", None, None, None),
        P("layer", None, None),
        P("layer", None, None),
        P("layer", None, None),
        P("layer", None, "row"),
        P("layer", None, None, "col"),
    )
    return jax.shard_map(
        on_device, mesh=mesh, in_specs=placed, out_specs=P("row", "layer", "col"), check_vma=False
    )
```

```python
import jax
import jax.numpy as jnp
from jax import lax
from jax.experimental import pallas as pl
from jax.experimental.pallas import tpu as pltpu
from jax.sharding import PartitionSpec as P

NZ, NX, NY = 4, 4, 8
NB = 256
SUB = 16
W = 1024
PANEL = 2 * W
CROSS = PANEL + 6 * NB
M0, M1, V, UI0, UI1, WW = (PANEL + i * NB for i in range(6))
COPIES = 128
F32, BF16 = jnp.float32, jnp.bfloat16


def dot(a, b):
    return jnp.dot(a, b, preferred_element_type=F32)


def dot_tn(a, b):
    return lax.dot_general(a, b, (((0,), (0,)), ((), ())), preferred_element_type=F32)


def dot_nt(a, b):
    return lax.dot_general(a, b, (((1,), (1,)), ((), ())), preferred_element_type=F32)


def kernel(trail_ref, *refs):
    body(trail_ref, refs[:9], refs[9], refs[10:19], *refs[19:])


def body(
    trail_ref, sources, out_ref, held,
    lo, xb, stage, uh, ub, own, masks, xmasks, lf, uf, acc, trail_v, out_v,
    send, recv, local,
):
    layer = lax.axis_index("layer")
    row = lax.axis_index("row")
    col = lax.axis_index("col")
    zl, x, y, core = row // NX, row % NX, col // 2, col % 2

    def at(dl=0, dz=0, dx=0, dy=0, k=None, mirror=False, dc=0):
        to_z = NZ - 1 - zl if mirror else (zl + dz + NZ) % NZ
        return (
            (layer + dl) % 2,
            to_z * NX + (x + dx + NX) % NX,
            (y + dy + NY) % NY * 2 + ((core + dc) % 2 if k is None else k),
        )

    def lslot(dy, k=None):
        first = (y + dy + NY) % NY * 2 * SUB
        if k is None:
            return pl.ds(pl.multiple_of(first, 2 * SUB), 2 * SUB)
        return pl.ds(pl.multiple_of(first + k * SUB, SUB), SUB)

    def uslot(i, dz, dx):
        first = i * NB + ((zl + dz + NZ) % NZ * NX + (x + dx + NX) % NX) * SUB
        return pl.ds(pl.multiple_of(first, SUB), SUB)

    barrier = pltpu.get_barrier_semaphore()

    def greet(**to):
        pl.semaphore_signal(barrier, 1, device_id=at(**to), device_id_type=pl.DeviceIdType.MESH)

    greet(dc=1)

    @pl.when(core == 0)
    def _():
        greet(dl=1, k=0)
        for k in range(2):
            greet(dx=1, k=k)
            greet(dx=-1, k=k)
            for j in (1, 2, 3):
                greet(dz=j, k=k)
            greet(dl=1, mirror=True, k=k)

    @pl.when(core == 1)
    def _():
        for k in range(2):
            greet(dy=1, k=k)
            greet(dy=-1, k=k)
            greet(dl=1, k=k)
        greet(dy=2, k=1)
        greet(dy=-2, k=1)

    lp_ref, up_ref, li_ref, ui_ref, above_ref, left_ref, order_ref, rmask_ref, cmask_ref = held
    loads = [
        pltpu.make_async_copy(src, dst, local.at[2 + i])
        for i, (src, dst) in enumerate(zip(sources, held))
    ]
    for copy in loads:
        copy.start()
    fetch = pltpu.make_async_copy(trail_ref, trail_v, local.at[0])
    fetch.start()

    loads[0].wait()
    loads[1].wait()
    for k in range(2):
        stage[:, pl.ds(k * W, W)] = lp_ref[k]
        for h in range(2):
            uh[h, :, pl.ds(k * W, W)] = up_ref[k, :, h, :]
    mine = lslot(0, core)
    lo[mine] = stage[:, :PANEL]
    lanes = pl.ds(pl.multiple_of(core * PANEL, PANEL), PANEL)

    ub[uslot(0, 0, 0), lanes] = uh[layer]
    for copy in loads[2:]:
        copy.wait()
    masks[...] = jnp.zeros_like(masks)
    masks[0:2, 0:4] = rmask_ref[...].astype(F32)
    for k in range(2):
        for h in range(2):
            r = 2 + 2 * h + k
            masks[r : r + 1, 0:4] = cmask_ref[k, h : h + 1, :].astype(F32)

    place = lax.broadcasted_iota(jnp.int32, (NB, NB), 0)

    def permuted(rows, k):
        hot = jnp.where(place == order_ref[k : k + 1, :], 1.0, 0.0).astype(BF16)
        return dot_nt(rows, hot).astype(BF16)

    share = mine
    m0 = permuted(li_ref[0, share], 0)
    m1 = permuted(li_ref[1, share], 1)
    lower_cross = dot(left_ref[...], ui_ref[0]).astype(BF16)
    upper_cross = dot(m0, above_ref[...]).astype(BF16)
    for place_at, value in (
        (M0, m0),
        (M1, m1),
        (V, dot(m1, lower_cross).astype(BF16)),
        (UI0, ui_ref[0, share]),
        (UI1, ui_ref[1, share]),
        (WW, dot(upper_cross, ui_ref[1]).astype(BF16)),
    ):
        stage[:, pl.ds(place_at, NB)] = value

    pl.semaphore_wait(barrier, 11 + core)

    names = {}

    def sem(name):
        return names.setdefault(name, len(names))

    def make(name, src, dst, index=None, **to):
        i = sem(name) if index is None else sem(name) + index
        return pltpu.make_async_remote_copy(
            src_ref=src, dst_ref=dst, send_sem=send.at[i], recv_sem=recv.at[i],
            device_id=at(**to), device_id_type=pl.DeviceIdType.MESH,
        )

    def pair(name):
        i = sem((name, 0))
        assert sem((name, 1)) == i + 1
        return (name, 0)

    def first(name, src, dst, **to):
        copy = make(pair(name), src, dst, index=core, **to)
        copy.start()
        return copy

    own_u, own_l = ub.at[uslot(0, 0, 0), lanes], lo.at[mine]
    begun = [
        first("p00", uh.at[layer], own_u, dx=1, k=0),
        first("m00", uh.at[layer], own_u, dx=-1, k=0),
        first("up1", own_l, own_l, dy=1, k=1),
        first("down1", own_l, own_l, dy=-1, k=1),
        first("z01", uh.at[layer], own_u, dz=1, k=0),
        first("z03", uh.at[layer], own_u, dz=3, k=0),
        first("cross", stage, xb.at[mine], dl=1, k=1),
        first("z02", uh.at[layer], own_u, dz=2, k=0),
        first("mirror", uh.at[1 - layer], ub.at[uslot(1, 0, 0), lanes], dl=1, mirror=True, k=0),
        first("sib", own_l, own_l, dc=1),
        first("masks", masks, xmasks, dl=1),
    ]

    def got(name, dst, k=None):
        index = None if k is None else k
        make(pair(name) if k is not None else name, dst, dst, index=index, dc=1).wait_recv()

    def go(list_, name, ref, **to):
        copy = make(name, ref, ref, **to)
        copy.start()
        list_.append(copy)

    def upper_work(steps):
        sent = []
        a, b = pl.ds(0, PANEL), pl.ds(PANEL, PANEL)

        def row_of(i, j, dx):
            if i == 0:
                return uslot(0, -j, dx)
            holder = (zl - j + NZ) % NZ
            first_row = NB + ((NZ - 1 - holder) * NX + (x + dx + NX) % NX) * SUB
            return pl.ds(pl.multiple_of(first_row, SUB), SUB)

        def spread(i, j):
            rows = row_of(i, j, 0)
            if i == 0:
                got(f"z0{j}", ub.at[rows, a], 0)
                got(f"z0{j}", ub.at[rows, b], 1)
            elif j == 0:
                got("mirror", ub.at[rows, a], 0)
                got("mirror", ub.at[rows, b], 1)
            else:
                got(("z1", j), ub.at[rows])
            go(sent, ("p", i, j), ub.at[rows], dx=1, k=0)
            go(sent, ("m", i, j), ub.at[rows], dx=-1, k=0)
            if i == 1 and j == 0:
                for d in (1, 3, 2):
                    go(sent, ("z1", d), ub.at[rows], dz=d, k=0)

        def forward(i, j):
            left, right = row_of(i, j, -1), row_of(i, j, 1)
            if (i, j) == (0, 0):
                got("p00", ub.at[left, a], 0)
            else:
                got(("p", i, j), ub.at[left])
            go(sent, ("f", i, j), ub.at[left, a], dx=1, k=0)
            if (i, j) == (0, 0):
                got("m00", ub.at[right, b], 1)
            else:
                got(("m", i, j), ub.at[right])
            go(sent, ("g", i, j), ub.at[right, b], dx=-1, k=0)

        def hand(i, j):
            far = row_of(i, j, 2)
            if (i, j) == (0, 0):
                got("p00", ub.at[row_of(0, 0, -1), b], 1)
                got("m00", ub.at[row_of(0, 0, 1), a], 0)
                for dx in (-1, 1):
                    go(sent, ("h", dx), ub.at[row_of(0, 0, dx), b], dc=1)
            got(("f", i, j), ub.at[far, a])
            got(("g", i, j), ub.at[far, b])
            if (i, j) == (0, 0):
                go(sent, ("h", 2), ub.at[far, b], dc=1)
            else:
                go(sent, ("h", i, j), ub.at[quad(i, j), b], dc=1)

        def quad(i, j):
            holder = (zl - j + NZ) % NZ
            base_row = i * NB + (holder if i == 0 else NZ - 1 - holder) * NX * SUB
            return pl.ds(pl.multiple_of(base_row, NX * SUB), NX * SUB)

        def lower_ready(i):
            buf = (lo, xb)[i]
            if i == 0:
                got("sib", lo.at[lslot(0, 1)], 1)
            for d in (0, 1, -1, 2, -2, 3, -3, 4):
                if i == 1 or d != 0:
                    got(("s", i, d), buf.at[lslot(d)])

        steps(spread, forward, hand, lower_ready)
        for copy in sent:
            copy.wait_send()

    def lower_work(steps):
        sent = []

        def pieces(i, s, d):
            buf = (lo, xb)[i]
            for k in range(2):
                rows = lslot(-s * d, k)
                if i == 0 and s == 1:
                    got("up1" if d == 1 else "down1", buf.at[rows], k)
                else:
                    got(("r", i, s, d, k), buf.at[rows])
                go(sent, ("r", i, s + 1, d, k), buf.at[rows], dy=d, k=1)
                if s == 2 and k == (0 if d == 1 else 1):
                    go(sent, ("far", i, d), buf.at[rows], dy=2 * d, k=1)
            go(sent, ("s", i, -s * d), buf.at[lslot(-s * d)], dc=1)

        def cross():
            for k in range(2):
                rows = lslot(0, k)
                got("cross", xb.at[rows], k)
                for d in (1, -1):
                    go(sent, ("r", 1, 1, d, k), xb.at[rows], dy=d, k=1)
            go(sent, ("s", 1, 0), xb.at[lslot(0)], dc=1)

        def step(i, s):
            for d in (1, -1):
                pieces(i, s, d)

        def last(i):
            buf = (lo, xb)[i]
            for d in (1, -1):
                for k in range(2):
                    got(("r", i, 3, d, k), buf.at[lslot(-3 * d, k)])
                go(sent, ("s", i, -3 * d), buf.at[lslot(-3 * d)], dc=1)
            for d, k in ((1, 0), (-1, 1)):
                got(("far", i, d), buf.at[lslot(4, k)])
            go(sent, ("s", i, 4), buf.at[lslot(4)], dc=1)

        def own_ready():
            got("sib", lo.at[lslot(0, 0)], 0)

        def upper_ready(i):
            b = pl.ds(PANEL, PANEL)
            for j in range(NZ):
                if (i, j) == (0, 0):
                    for dx in (-1, 1, 2):
                        got(("h", dx), ub.at[uslot(0, 0, dx), b])
                    continue
                holder = (zl - j + NZ) % NZ
                base_row = i * NB + (holder if i == 0 else NZ - 1 - holder) * NX * SUB
                got(("h", i, j), ub.at[pl.ds(pl.multiple_of(base_row, NX * SUB), NX * SUB), b])

        steps(cross, step, last, own_ready, upper_ready)
        for copy in sent:
            copy.wait_send()

    def own_small():
        own[0] = permuted(li_ref[0], 0)
        own[1] = permuted(li_ref[1], 1)
        own[2] = dot(own[1], lower_cross).astype(BF16)
        own[3] = dot(dot(own[0], above_ref[...]).astype(BF16), ui_ref[1]).astype(BF16)

    def lower_factors(i, b):
        if i == 0:
            buf, ui0, ui1, w, mask = lo, ui_ref[0], ui_ref[1], own[3], masks
        else:
            buf, mask = xb, xmasks
            ui0, ui1, w = (xb[:, pl.ds(c, NB)] for c in (UI0, UI1, WW))
        rows = pl.ds(b * NB, NB)
        first = (dot_tn(buf[:, pl.ds(b * NB, NB)], ui0) * mask[0:1, b : b + 1]).astype(BF16)
        second = dot_tn(buf[:, pl.ds(W + b * NB, NB)], ui1) - dot(first, w)
        lf[i, rows, 0:NB] = first
        lf[i, rows, NB : 2 * NB] = (second * mask[1:2, b : b + 1]).astype(BF16)

    def upper_factors(i, b):
        rows = pl.ds(i * NB, NB)
        if i == 0:
            m0, m1, v, mask = own[0], own[1], own[2], masks
        else:
            mask = xmasks
            m0, m1, v = (xb[:, pl.ds(c, NB)] for c in (M0, M1, V))
        c0 = mask[pl.ds(2 + 2 * layer, 1), :]
        c1 = mask[pl.ds(3 + 2 * layer, 1), :]
        cols = pl.ds(b * NB, NB)
        at0 = pl.ds(pl.multiple_of(core * PANEL + b * NB, NB), NB)
        at1 = pl.ds(pl.multiple_of(core * PANEL + W + b * NB, NB), NB)
        first = (dot(m0, ub[rows, at0]) * c0[:, b : b + 1]).astype(BF16)
        second = dot(m1, ub[rows, at1]) - dot(v, first)
        uf[i, 0:NB, cols] = first
        uf[i, NB : 2 * NB, cols] = (second * c1[:, b : b + 1]).astype(BF16)

    def product(i, b):
        return dot(lf[i, pl.ds(b * NB, NB)], uf[i])

    def base():
        @pl.loop(0, 4)
        def _(b):
            rows = pl.ds(pl.multiple_of(b * NB, NB), NB)
            acc[rows] = product(0, b)

    def finish():
        @pl.loop(0, 4)
        def _(b):
            rows = pl.ds(pl.multiple_of(b * NB, NB), NB)
            total = acc[rows] + product(1, b)
            out_v[rows] = (trail_v[rows].astype(F32) - total).astype(BF16)

    @pl.when(core == 0)
    def _():
        def steps(spread, forward, hand, lower_ready):
            forward(0, 0)
            spread(0, 1)
            spread(0, 3)
            spread(0, 2)
            own_small()
            forward(0, 1)
            spread(1, 0)
            hand(0, 0)
            forward(0, 3)
            forward(0, 2)
            forward(1, 0)
            hand(0, 1)
            spread(1, 1)
            spread(1, 3)
            hand(0, 3)
            spread(1, 2)
            hand(0, 2)
            lower_ready(0)
            for b in range(4):
                lower_factors(0, b)
            forward(1, 1)
            forward(1, 3)
            hand(1, 0)
            forward(1, 2)
            for b in range(4):
                upper_factors(0, b)
            hand(1, 1)
            hand(1, 3)
            hand(1, 2)
            base()
            lower_ready(1)

        upper_work(steps)

    @pl.when(core == 1)
    def _():
        def steps(cross, step, last, own_ready, upper_ready):
            own_ready()
            step(0, 1)
            own_small()
            step(0, 2)
            cross()
            last(0)
            step(1, 1)
            for b in range(4):
                lower_factors(0, b)
            step(1, 2)
            upper_ready(0)
            for b in range(4):
                upper_factors(0, b)
            last(1)
            base()
            upper_ready(1)

        lower_work(steps)

    got("masks", xmasks, core)
    for b in range(4):
        lower_factors(1, b)
    for b in range(4):
        upper_factors(1, b)
    fetch.wait()
    finish()

    put = pltpu.make_async_copy(out_v, out_ref, local.at[1])
    put.start()
    for copy in begun:
        copy.wait_send()
    put.wait()


def on_device(trail, lower, upper, li, ui, above, left, order, rmask, cmask):
    operands = (lower[0], upper[0], li[0], ui[0], above[0], left[0], order[0], rmask[0], cmask[0])
    hbm = pl.BlockSpec(memory_space=pltpu.HBM)
    out = pl.pallas_call(
        kernel,
        out_shape=jax.ShapeDtypeStruct((W, W), BF16),
        in_specs=[hbm] * 10,
        out_specs=pl.BlockSpec(memory_space=pl.ANY),
        scratch_shapes=[pltpu.VMEM(a.shape, a.dtype) for a in operands]
        + [
            pltpu.VMEM((NB, PANEL), BF16),
            pltpu.VMEM((NB, CROSS), BF16),
            pltpu.VMEM((SUB, CROSS), BF16),
            pltpu.VMEM((2, SUB, PANEL), BF16),
            pltpu.VMEM((2 * NB, 2 * PANEL), BF16),
            pltpu.VMEM((4, NB, NB), BF16),
            pltpu.VMEM((8, 128), F32),
            pltpu.VMEM((8, 128), F32),
            pltpu.VMEM((2, W, 2 * NB), BF16),
            pltpu.VMEM((2, 2 * NB, W), BF16),
            pltpu.VMEM((W, W), F32),
            pltpu.VMEM((W, W), BF16),
            pltpu.VMEM((W, W), BF16),
            pltpu.SemaphoreType.DMA((COPIES,)),
            pltpu.SemaphoreType.DMA((COPIES,)),
            pltpu.SemaphoreType.DMA((11,)),
        ],
        compiler_params=pltpu.CompilerParams(
            collective_id=0, has_side_effects=True, vmem_limit_bytes=60 * 2**20
        ),
        name="panels_update",
    )(trail[:, 0, :], *operands)
    return out[:, None, :]


def solution(mesh):
    placed = (
        P("row", "layer", "col"),
        P("layer", None, "col", "row"),
        P("layer", None, "row", None, "col"),
        P("layer", None, None, None),
        P("layer", None, None, None),
        P("layer", None, None),
        P("layer", None, None),
        P("layer", None, None),
        P("layer", None, "row"),
        P("layer", None, None, "col"),
    )
    return jax.shard_map(
        on_device, mesh=mesh, in_specs=placed, out_specs=P("row", "layer", "col"), check_vma=False
    )
```

```python
import jax
import jax.numpy as jnp
from jax import lax
from jax.experimental import pallas as pl
from jax.experimental.pallas import tpu as pltpu
from jax.sharding import PartitionSpec as P

NZ, NX, NY = 8, 4, 8
LZ = NZ // 2
NB = 256
SUB = 16
W = 1024
PANEL = 2 * W
CROSS = PANEL + 6 * NB
M0, M1, V, UI0, UI1, WW = (PANEL + i * NB for i in range(6))
COPIES = 128
DIRECT = (4,)
F32, BF16 = jnp.float32, jnp.bfloat16


def dot(a, b):
    return jnp.dot(a, b, preferred_element_type=F32)


def dot_tn(a, b):
    return lax.dot_general(a, b, (((0,), (0,)), ((), ())), preferred_element_type=F32)


def dot_nt(a, b):
    return lax.dot_general(a, b, (((1,), (1,)), ((), ())), preferred_element_type=F32)


def kernel(trail_ref, *refs):
    body(trail_ref, refs[:9], refs[9], refs[10:19], *refs[19:])


def body(
    trail_ref, sources, out_ref, held,
    lo, xb, stage, uh, uu, own, masks, xmasks, lf, uf, trail_v, out_v,
    send, recv, local,
):
    layer = lax.axis_index("layer")
    row = lax.axis_index("row")
    col = lax.axis_index("col")
    z, x, y, core = layer * LZ + row // NX, row % NX, col // 2, col % 2

    def at(dz=0, dx=0, dy=0, dc=0, k=None):
        to = (z + dz + NZ) % NZ
        return (
            to // LZ,
            to % LZ * NX + (x + dx + NX) % NX,
            (y + dy + NY) % NY * 2 + ((core + dc) % 2 if k is None else k),
        )

    def half_of(dz):
        return (z + dz + NZ) % NZ // LZ

    def lslot(dy, k=None):
        start = (y + dy + NY) % NY * 2 * SUB
        if k is None:
            return pl.ds(pl.multiple_of(start, 2 * SUB), 2 * SUB)
        return pl.ds(pl.multiple_of(start + k * SUB, SUB), SUB)

    def uslot(dz, dx=0):
        at_row = ((z + dz + NZ) % NZ * NX + (x + dx + NX) % NX) * SUB
        return pl.ds(pl.multiple_of(at_row, SUB), SUB)

    lp_ref, up_ref, li_ref, ui_ref, above_ref, left_ref, order_ref, rmask_ref, cmask_ref = held
    loads = [
        pltpu.make_async_copy(src, dst, local.at[2 + i])
        for i, (src, dst) in enumerate(zip(sources, held))
    ]
    for copy in loads:
        copy.start()
    barrier = pltpu.get_barrier_semaphore()

    def greet(**to):
        pl.semaphore_signal(barrier, 1, device_id=at(**to), device_id_type=pl.DeviceIdType.MESH)

    for d in (1, -1):
        greet(dx=d)
        greet(dz=d)
        greet(dz=2 * d)
        greet(dy=d)
        greet(dy=2 * d)
    greet(dc=1)
    greet(dz=4)
    greet(dx=2)

    @pl.when(core == 0)
    def _():
        greet(dy=1, k=1)
        greet(dy=-1, k=1)

    @pl.when(core == 1)
    def _():
        greet(dz=4, k=0)

    fetch = pltpu.make_async_copy(trail_ref, trail_v, local.at[0])
    fetch.start()

    loads[0].wait()
    loads[1].wait()
    for k in range(2):
        stage[:, pl.ds(k * W, W)] = lp_ref[k]
        for h in range(2):
            uh[h, :, pl.ds(k * W, W)] = up_ref[k, :, h, :]
    share = lslot(0, core)
    lo[share] = stage[:, :PANEL]
    uu[layer, uslot(0)] = uh[layer]
    pl.semaphore_wait(barrier, 14 + core)

    names = {}
    begun = []

    def sem(name):
        return names.setdefault(name, len(names))

    def make(name, src, dst, index=None, **to):
        if index is None:
            i = sem(name)
        else:
            i = sem((name, 0))
            assert sem((name, 1)) == i + 1
            i = i + index
        return pltpu.make_async_remote_copy(
            src_ref=src, dst_ref=dst, send_sem=send.at[i], recv_sem=recv.at[i],
            device_id=at(**to), device_id_type=pl.DeviceIdType.MESH,
        )

    def go(sent, name, src, dst=None, **to):
        copy = make(name, src, src if dst is None else dst, **to)
        copy.start()
        sent.append(copy)

    def got(name, dst, index=None):
        make(name, dst, dst, index=index, dc=1).wait_recv()

    def zpart(dz, half, i=None):
        if i is None:
            return uu.at[half, uslot(dz)]
        return uu.at[half, uslot(dz), pl.ds(i * W, W)]

    own_l = lo.at[share]

    go(begun, ("p", 0), zpart(0, layer), dx=1)
    go(begun, ("m", 0), zpart(0, layer), dx=-1)
    for other in (0, 1):
        for d in (1, -1):
            h = (half_of(d) + other) % 2
            go(begun, ("z", d, other), uh.at[h], zpart(0, h), dz=d)
        if other == 0:
            go(begun, "up1", own_l, index=core, dy=1, k=0)
            go(begun, "down1", own_l, index=core, dy=-1, k=0)
    go(begun, "sib", own_l, index=core, dc=1)
    for copy in loads[2:]:
        copy.wait()
    masks[...] = jnp.zeros_like(masks)
    masks[0:2, 0:4] = rmask_ref[...].astype(F32)
    for k in range(2):
        for h in range(2):
            r = 2 + 2 * h + k
            masks[r : r + 1, 0:4] = cmask_ref[k, h : h + 1, :].astype(F32)

    place = lax.broadcasted_iota(jnp.int32, (NB, NB), 0)

    def permuted(rows, k):
        hot = jnp.where(place == order_ref[k : k + 1, :], 1.0, 0.0).astype(BF16)
        return dot_nt(rows, hot).astype(BF16)

    m0 = permuted(li_ref[0, share], 0)
    m1 = permuted(li_ref[1, share], 1)
    lower_cross = dot(left_ref[...], ui_ref[0]).astype(BF16)
    upper_cross = dot(m0, above_ref[...]).astype(BF16)
    for place_at, value in (
        (M0, m0),
        (M1, m1),
        (V, dot(m1, lower_cross).astype(BF16)),
        (UI0, ui_ref[0, share]),
        (UI1, ui_ref[1, share]),
        (WW, dot(upper_cross, ui_ref[1]).astype(BF16)),
    ):
        stage[:, pl.ds(place_at, NB)] = value

    go(begun, "cross", stage, xb.at[share], index=core, dz=4, k=1)
    go(begun, "masks", masks, xmasks, dz=4)

    class Plane:
        def __init__(self, sent):
            self.sent = sent

        def hop2(self):
            for other in (0, 1):
                for d in (1, -1):
                    if other == 0:
                        got(("z", d, 1), zpart(-d, 1 - layer))
                    h = (half_of(d) + other) % 2
                    go(self.sent, ("z", 2 * d, other), zpart(-d, h), dz=d)

        def hop3(self):
            for d in (1, -1):
                got(("z", 2 * d, 1), zpart(-2 * d, 1 - layer))
                go(self.sent, ("z", 3 * d, 0), zpart(-2 * d, half_of(d)), dz=d)
                part = zpart(-2 * d, half_of(2 * d), 0 if d == 1 else 1)
                go(self.sent, ("z", 4 * d, 0), part, dz=2 * d)

        def spread(self, *ds):
            for d in ds:
                if d == 4:
                    got(("z", 4, 0), zpart(-4, layer, 0))
                    got(("z", -4, 0), zpart(4, layer, 1))
                else:
                    got(("z", d, 0), zpart(-d, layer))
                go(self.sent, ("p", d), zpart(-d, layer), dx=1)
                go(self.sent, ("m", d), zpart(-d, layer), dx=-1)
                if d in DIRECT:
                    go(self.sent, ("q", d), zpart(-d, layer), dx=2)

        def forward(self, *ds):
            for d in ds:
                left, right = uslot(-d, -1), uslot(-d, 1)
                got(("p", d), uu.at[layer, left])
                if d not in DIRECT:
                    go(self.sent, ("f", d), uu.at[layer, left, pl.ds(0, W)], dx=1)
                got(("m", d), uu.at[layer, right])
                if d not in DIRECT:
                    go(self.sent, ("g", d), uu.at[layer, right, pl.ds(W, W)], dx=-1)

        def end(self):
            for d in (0, 1, -1, 2, -2, 3, -3, 4):
                if d in DIRECT:
                    got(("q", d), uu.at[layer, uslot(-d, 2)])
                    continue
                got(("f", d), uu.at[layer, uslot(-d, 2), pl.ds(0, W)])
                got(("g", d), uu.at[layer, uslot(-d, 2), pl.ds(W, W)])

    class Ring:
        def __init__(self, sent, i):
            self.sent, self.i, self.buf = sent, i, (lo, xb)[i]

        def hand(self, d):
            go(self.sent, ("s", self.i, d), self.buf.at[lslot(d)], dc=1)

        def cross(self):
            for k in range(2):
                rows = self.buf.at[lslot(0, k)]
                got("cross", rows, k)
                for d in (1, -1):
                    go(self.sent, ("r", 1, 1, d, k), rows, dy=d)
            self.hand(0)

        def step(self, s):
            for k in range(2):
                for d in (1, -1):
                    rows = self.buf.at[lslot(-s * d, k)]
                    if self.i == 0 and s == 1:
                        got("up1" if d == 1 else "down1", rows, k)
                    else:
                        got(("r", self.i, s, d, k), rows)
                    go(self.sent, ("r", self.i, s + 1, d, k), rows, dy=d)
                    if s == 2 and k == (0 if d == 1 else 1):
                        go(self.sent, ("far", self.i, d), rows, dy=2 * d)
            self.hand(-s)
            self.hand(s)

        def last(self):
            for d in (1, -1):
                for k in range(2):
                    got(("r", self.i, 3, d, k), self.buf.at[lslot(-3 * d, k)])
                self.hand(-3 * d)
            for d, k in ((1, 0), (-1, 1)):
                got(("far", self.i, d), self.buf.at[lslot(4, k)])
            self.hand(4)

    def lower_ready(i):
        for d in (0, 1, -1, 2, -2, 3, -3, 4):
            if i == 1 or d != 0:
                got(("s", i, d), (lo, xb)[i].at[lslot(d)])

    def own_small():
        own[0] = permuted(li_ref[0], 0)
        own[1] = permuted(li_ref[1], 1)
        own[2] = dot(own[1], lower_cross).astype(BF16)
        own[3] = dot(dot(own[0], above_ref[...]).astype(BF16), ui_ref[1]).astype(BF16)

    def lower_factors(i, b):
        if i == 0:
            buf, ui0, ui1, w, mask = lo, ui_ref[0], ui_ref[1], own[3], masks
        else:
            buf, mask = xb, xmasks
            ui0, ui1, w = (xb[:, pl.ds(c, NB)] for c in (UI0, UI1, WW))
        rows = pl.ds(b * NB, NB)
        first = (dot_tn(buf[:, pl.ds(b * NB, NB)], ui0) * mask[0:1, b : b + 1]).astype(BF16)
        second = dot_tn(buf[:, pl.ds(W + b * NB, NB)], ui1) - dot(first, w)
        lf[i, rows, 0:NB] = first
        lf[i, rows, NB : 2 * NB] = (second * mask[1:2, b : b + 1]).astype(BF16)

    def upper_factors(i, b):
        rows = pl.ds(pl.multiple_of((layer if i == 0 else 1 - layer) * NB, NB), NB)
        if i == 0:
            m0, m1, v, mask = own[0], own[1], own[2], masks
        else:
            mask = xmasks
            m0, m1, v = (xb[:, pl.ds(c, NB)] for c in (M0, M1, V))
        c0 = mask[pl.ds(2 + 2 * layer, 1), :]
        c1 = mask[pl.ds(3 + 2 * layer, 1), :]
        cols = pl.ds(b * NB, NB)
        first = (dot(m0, uu[layer, rows, cols]) * c0[:, b : b + 1]).astype(BF16)
        second = dot(m1, uu[layer, rows, pl.ds(W + b * NB, NB)]) - dot(v, first)
        uf[i, 0:NB, cols] = first
        uf[i, NB : 2 * NB, cols] = (second * c1[:, b : b + 1]).astype(BF16)

    def product(i, b):
        return dot(lf[i, pl.ds(b * NB, NB)], uf[i])

    def finish():
        @pl.loop(0, 4)
        def _(b):
            rows = pl.ds(pl.multiple_of(b * NB, NB), NB)
            total = product(0, b) + product(1, b)
            out_v[rows] = (trail_v[rows].astype(F32) - total).astype(BF16)
            pltpu.make_async_copy(out_v.at[rows], out_ref.at[rows], local.at[1]).start()

    @pl.when(core == 0)
    def _():
        sent = []
        U, L = Plane(sent), Ring(sent, 0)
        U.forward(0)
        U.spread(1, -1)
        L.step(1)
        U.hop2()
        own_small()
        L.step(2)
        U.forward(1, -1)
        U.spread(2, -2)
        U.hop3()
        U.forward(2, -2)
        L.last()
        got("sib", lo.at[lslot(0, 1)], 1)
        U.spread(3, -3)
        U.spread(4)
        for b in range(4):
            lower_factors(0, b)
        U.forward(3, -3, 4)
        lower_ready(1)
        got("masks", xmasks)
        for b in range(4):
            lower_factors(1, b)
        U.end()
        for copy in sent:
            copy.wait_send()

    @pl.when(core == 1)
    def _():
        sent = []
        U, L = Plane(sent), Ring(sent, 1)
        U.forward(0)
        U.spread(1, -1)
        U.hop2()
        own_small()
        L.cross()
        U.forward(1, -1)
        U.spread(2, -2)
        U.hop3()
        L.step(1)
        U.forward(2, -2)
        got("sib", lo.at[lslot(0, 0)], 0)
        U.spread(3, -3)
        U.spread(4)
        L.step(2)
        lower_ready(0)
        for b in range(4):
            lower_factors(0, b)
        U.forward(3, -3, 4)
        L.last()
        got("masks", xmasks)
        for b in range(4):
            lower_factors(1, b)
        U.end()
        for copy in sent:
            copy.wait_send()

    for b in range(4):
        upper_factors(0, b)
    for b in range(4):
        upper_factors(1, b)
    fetch.wait()
    finish()

    for copy in begun:
        copy.wait_send()
    pltpu.make_async_copy(out_v, out_ref, local.at[1]).wait()


def on_device(trail, lower, upper, li, ui, above, left, order, rmask, cmask):
    operands = (lower[0], upper[0], li[0], ui[0], above[0], left[0], order[0], rmask[0], cmask[0])
    hbm = pl.BlockSpec(memory_space=pltpu.HBM)
    out = pl.pallas_call(
        kernel,
        out_shape=jax.ShapeDtypeStruct((W, W), BF16),
        in_specs=[hbm] * 10,
        out_specs=pl.BlockSpec(memory_space=pl.ANY),
        scratch_shapes=[pltpu.VMEM(a.shape, a.dtype) for a in operands]
        + [
            pltpu.VMEM((NB, PANEL), BF16),
            pltpu.VMEM((NB, CROSS), BF16),
            pltpu.VMEM((SUB, CROSS), BF16),
            pltpu.VMEM((2, SUB, PANEL), BF16),
            pltpu.VMEM((2, 2 * NB, PANEL), BF16),
            pltpu.VMEM((4, NB, NB), BF16),
            pltpu.VMEM((8, 128), F32),
            pltpu.VMEM((8, 128), F32),
            pltpu.VMEM((2, W, 2 * NB), BF16),
            pltpu.VMEM((2, 2 * NB, W), BF16),
            pltpu.VMEM((W, W), BF16),
            pltpu.VMEM((W, W), BF16),
            pltpu.SemaphoreType.DMA((COPIES,)),
            pltpu.SemaphoreType.DMA((COPIES,)),
            pltpu.SemaphoreType.DMA((11,)),
        ],
        compiler_params=pltpu.CompilerParams(
            collective_id=0, has_side_effects=True, vmem_limit_bytes=60 * 2**20
        ),
        name="panels_update",
    )(trail[:, 0, :], *operands)
    return out[:, None, :]


def solution(mesh):
    placed = (
        P("row", "layer", "col"),
        P("layer", None, "col", "row"),
        P("layer", None, "row", None, "col"),
        P("layer", None, None, None),
        P("layer", None, None, None),
        P("layer", None, None),
        P("layer", None, None),
        P("layer", None, None),
        P("layer", None, "row"),
        P("layer", None, None, "col"),
    )
    return jax.shard_map(
        on_device, mesh=mesh, in_specs=placed, out_specs=P("row", "layer", "col"), check_vma=False
    )
```

```python
import jax
import jax.numpy as jnp
from jax import lax
from jax.experimental import pallas as pl
from jax.experimental.pallas import tpu as pltpu
from jax.sharding import PartitionSpec as P

NZ, NX, NY = 8, 4, 8
LZ = NZ // 2
NB = 256
SUB = 16
W = 1024
PANEL = 2 * W
CROSS = PANEL + 6 * NB
M0, M1, V, UI0, UI1, WW = (PANEL + i * NB for i in range(6))
COPIES = 128
DIRECT = (4,)
F32, BF16 = jnp.float32, jnp.bfloat16


def dot(a, b):
    return jnp.dot(a, b, preferred_element_type=F32)


def dot_tn(a, b):
    return lax.dot_general(a, b, (((0,), (0,)), ((), ())), preferred_element_type=F32)


def dot_nt(a, b):
    return lax.dot_general(a, b, (((1,), (1,)), ((), ())), preferred_element_type=F32)


def kernel(trail_ref, *refs):
    body(trail_ref, refs[:9], refs[9], refs[10:19], *refs[19:])


def body(
    trail_ref, sources, out_ref, held,
    lo, xb, stage, uh, uu, own, masks, xmasks, lf, uf, acc, trail_v, out_v,
    send, recv, local,
):
    layer = lax.axis_index("layer")
    row = lax.axis_index("row")
    col = lax.axis_index("col")
    z, x, y, core = layer * LZ + row // NX, row % NX, col // 2, col % 2

    def at(dz=0, dx=0, dy=0, dc=0, k=None):
        to = (z + dz + NZ) % NZ
        return (
            to // LZ,
            to % LZ * NX + (x + dx + NX) % NX,
            (y + dy + NY) % NY * 2 + ((core + dc) % 2 if k is None else k),
        )

    def half_of(dz):
        return (z + dz + NZ) % NZ // LZ

    def lslot(dy, k=None):
        start = (y + dy + NY) % NY * 2 * SUB
        if k is None:
            return pl.ds(pl.multiple_of(start, 2 * SUB), 2 * SUB)
        return pl.ds(pl.multiple_of(start + k * SUB, SUB), SUB)

    def uslot(dz, dx=0):
        at_row = ((z + dz + NZ) % NZ * NX + (x + dx + NX) % NX) * SUB
        return pl.ds(pl.multiple_of(at_row, SUB), SUB)

    lp_ref, up_ref, li_ref, ui_ref, above_ref, left_ref, order_ref, rmask_ref, cmask_ref = held
    loads = [
        pltpu.make_async_copy(src, dst, local.at[2 + i])
        for i, (src, dst) in enumerate(zip(sources, held))
    ]
    for copy in loads:
        copy.start()
    barrier = pltpu.get_barrier_semaphore()

    def greet(**to):
        pl.semaphore_signal(barrier, 1, device_id=at(**to), device_id_type=pl.DeviceIdType.MESH)

    for d in (1, -1):
        greet(dx=d)
        greet(dz=d)
        greet(dz=2 * d)
        greet(dy=d)
        greet(dy=2 * d)
    greet(dc=1)
    greet(dz=4)
    greet(dx=2)

    @pl.when(core == 0)
    def _():
        greet(dy=1, k=1)
        greet(dy=-1, k=1)

    @pl.when(core == 1)
    def _():
        greet(dz=4, k=0)

    fetch = pltpu.make_async_copy(trail_ref, trail_v, local.at[0])
    fetch.start()

    loads[0].wait()
    loads[1].wait()
    for k in range(2):
        stage[:, pl.ds(k * W, W)] = lp_ref[k]
        for h in range(2):
            uh[h, :, pl.ds(k * W, W)] = up_ref[k, :, h, :]
    share = lslot(0, core)
    lo[share] = stage[:, :PANEL]
    uu[layer, uslot(0)] = uh[layer]
    pl.semaphore_wait(barrier, 14 + core)

    names = {}
    begun = []

    def sem(name):
        return names.setdefault(name, len(names))

    def make(name, src, dst, index=None, **to):
        if index is None:
            i = sem(name)
        else:
            i = sem((name, 0))
            assert sem((name, 1)) == i + 1
            i = i + index
        return pltpu.make_async_remote_copy(
            src_ref=src, dst_ref=dst, send_sem=send.at[i], recv_sem=recv.at[i],
            device_id=at(**to), device_id_type=pl.DeviceIdType.MESH,
        )

    def go(sent, name, src, dst=None, **to):
        copy = make(name, src, src if dst is None else dst, **to)
        copy.start()
        sent.append(copy)

    def got(name, dst, index=None):
        make(name, dst, dst, index=index, dc=1).wait_recv()

    def zpart(dz, half, i=None):
        if i is None:
            return uu.at[half, uslot(dz)]
        return uu.at[half, uslot(dz), pl.ds(i * W, W)]

    own_l = lo.at[share]

    go(begun, ("p", 0), zpart(0, layer), dx=1)
    go(begun, ("m", 0), zpart(0, layer), dx=-1)
    for other in (0, 1):
        for d in (1, -1):
            h = (half_of(d) + other) % 2
            go(begun, ("z", d, other), uh.at[h], zpart(0, h), dz=d)
        if other == 0:
            go(begun, "up1", own_l, index=core, dy=1, k=0)
            go(begun, "down1", own_l, index=core, dy=-1, k=0)
    go(begun, "sib", own_l, index=core, dc=1)
    for copy in loads[2:]:
        copy.wait()
    masks[...] = jnp.zeros_like(masks)
    masks[0:2, 0:4] = rmask_ref[...].astype(F32)
    for k in range(2):
        for h in range(2):
            r = 2 + 2 * h + k
            masks[r : r + 1, 0:4] = cmask_ref[k, h : h + 1, :].astype(F32)

    place = lax.broadcasted_iota(jnp.int32, (NB, NB), 0)

    def permuted(rows, k):
        hot = jnp.where(place == order_ref[k : k + 1, :], 1.0, 0.0).astype(BF16)
        return dot_nt(rows, hot).astype(BF16)

    m0 = permuted(li_ref[0, share], 0)
    m1 = permuted(li_ref[1, share], 1)
    lower_cross = dot(left_ref[...], ui_ref[0]).astype(BF16)
    upper_cross = dot(m0, above_ref[...]).astype(BF16)
    for place_at, value in (
        (M0, m0),
        (M1, m1),
        (V, dot(m1, lower_cross).astype(BF16)),
        (UI0, ui_ref[0, share]),
        (UI1, ui_ref[1, share]),
        (WW, dot(upper_cross, ui_ref[1]).astype(BF16)),
    ):
        stage[:, pl.ds(place_at, NB)] = value

    go(begun, "cross", stage, xb.at[share], index=core, dz=4, k=1)
    go(begun, "masks", masks, xmasks, dz=4)

    class Plane:
        def __init__(self, sent):
            self.sent = sent

        def hop2(self):
            for other in (0, 1):
                for d in (1, -1):
                    if other == 0:
                        got(("z", d, 1), zpart(-d, 1 - layer))
                    h = (half_of(d) + other) % 2
                    go(self.sent, ("z", 2 * d, other), zpart(-d, h), dz=d)

        def hop3(self):
            for d in (1, -1):
                got(("z", 2 * d, 1), zpart(-2 * d, 1 - layer))
                go(self.sent, ("z", 3 * d, 0), zpart(-2 * d, half_of(d)), dz=d)
                part = zpart(-2 * d, half_of(2 * d), 0 if d == 1 else 1)
                go(self.sent, ("z", 4 * d, 0), part, dz=2 * d)

        def spread(self, *ds):
            for d in ds:
                if d == 4:
                    got(("z", 4, 0), zpart(-4, layer, 0))
                    got(("z", -4, 0), zpart(4, layer, 1))
                else:
                    got(("z", d, 0), zpart(-d, layer))
                go(self.sent, ("p", d), zpart(-d, layer), dx=1)
                go(self.sent, ("m", d), zpart(-d, layer), dx=-1)
                if d in DIRECT:
                    go(self.sent, ("q", d), zpart(-d, layer), dx=2)

        def forward(self, *ds):
            for d in ds:
                left, right = uslot(-d, -1), uslot(-d, 1)
                got(("p", d), uu.at[layer, left])
                if d not in DIRECT:
                    go(self.sent, ("f", d), uu.at[layer, left, pl.ds(0, W)], dx=1)
                got(("m", d), uu.at[layer, right])
                if d not in DIRECT:
                    go(self.sent, ("g", d), uu.at[layer, right, pl.ds(W, W)], dx=-1)

        def end(self, *ds):
            for d in ds:
                if d in DIRECT:
                    got(("q", d), uu.at[layer, uslot(-d, 2)])
                    continue
                got(("f", d), uu.at[layer, uslot(-d, 2), pl.ds(0, W)])
                got(("g", d), uu.at[layer, uslot(-d, 2), pl.ds(W, W)])

    class Ring:
        def __init__(self, sent, i):
            self.sent, self.i, self.buf = sent, i, (lo, xb)[i]

        def hand(self, d):
            go(self.sent, ("s", self.i, d), self.buf.at[lslot(d)], dc=1)

        def cross(self):
            for k in range(2):
                rows = self.buf.at[lslot(0, k)]
                got("cross", rows, k)
                for d in (1, -1):
                    go(self.sent, ("r", 1, 1, d, k), rows, dy=d)
            self.hand(0)

        def step(self, s):
            for k in range(2):
                for d in (1, -1):
                    rows = self.buf.at[lslot(-s * d, k)]
                    if self.i == 0 and s == 1:
                        got("up1" if d == 1 else "down1", rows, k)
                    else:
                        got(("r", self.i, s, d, k), rows)
                    go(self.sent, ("r", self.i, s + 1, d, k), rows, dy=d)
                    if s == 2 and k == (0 if d == 1 else 1):
                        go(self.sent, ("far", self.i, d), rows, dy=2 * d)
            self.hand(-s)
            self.hand(s)

        def last(self):
            for d in (1, -1):
                for k in range(2):
                    got(("r", self.i, 3, d, k), self.buf.at[lslot(-3 * d, k)])
                self.hand(-3 * d)
            for d, k in ((1, 0), (-1, 1)):
                got(("far", self.i, d), self.buf.at[lslot(4, k)])
            self.hand(4)

    def lower_ready(i):
        for d in (0, 1, -1, 2, -2, 3, -3, 4):
            if i == 1 or d != 0:
                got(("s", i, d), (lo, xb)[i].at[lslot(d)])

    def own_small():
        own[0] = permuted(li_ref[0], 0)
        own[1] = permuted(li_ref[1], 1)
        own[2] = dot(own[1], lower_cross).astype(BF16)
        own[3] = dot(dot(own[0], above_ref[...]).astype(BF16), ui_ref[1]).astype(BF16)

    def lower_factors(i, b):
        if i == 0:
            buf, ui0, ui1, w, mask = lo, ui_ref[0], ui_ref[1], own[3], masks
        else:
            buf, mask = xb, xmasks
            ui0, ui1, w = (xb[:, pl.ds(c, NB)] for c in (UI0, UI1, WW))
        rows = pl.ds(b * NB, NB)
        first = (dot_tn(buf[:, pl.ds(b * NB, NB)], ui0) * mask[0:1, b : b + 1]).astype(BF16)
        second = dot_tn(buf[:, pl.ds(W + b * NB, NB)], ui1) - dot(first, w)
        lf[i, rows, 0:NB] = first
        lf[i, rows, NB : 2 * NB] = (second * mask[1:2, b : b + 1]).astype(BF16)

    def upper_factors(i, b):
        rows = pl.ds(pl.multiple_of((layer if i == 0 else 1 - layer) * NB, NB), NB)
        if i == 0:
            m0, m1, v, mask = own[0], own[1], own[2], masks
        else:
            mask = xmasks
            m0, m1, v = (xb[:, pl.ds(c, NB)] for c in (M0, M1, V))
        c0 = mask[pl.ds(2 + 2 * layer, 1), :]
        c1 = mask[pl.ds(3 + 2 * layer, 1), :]
        cols = pl.ds(b * NB, NB)
        first = (dot(m0, uu[layer, rows, cols]) * c0[:, b : b + 1]).astype(BF16)
        second = dot(m1, uu[layer, rows, pl.ds(W + b * NB, NB)]) - dot(v, first)
        uf[i, 0:NB, cols] = first
        uf[i, NB : 2 * NB, cols] = (second * c1[:, b : b + 1]).astype(BF16)

    def product(i, b):
        return dot(lf[i, pl.ds(b * NB, NB)], uf[i])

    def base():
        @pl.loop(0, 4)
        def _(b):
            acc[pl.ds(pl.multiple_of(b * NB, NB), NB)] = product(0, b)

    def finish():
        @pl.loop(0, 4)
        def _(b):
            rows = pl.ds(pl.multiple_of(b * NB, NB), NB)
            total = acc[rows] + product(1, b)
            out_v[rows] = (trail_v[rows].astype(F32) - total).astype(BF16)
            pltpu.make_async_copy(out_v.at[rows], out_ref.at[rows], local.at[1]).start()

    @pl.when(core == 0)
    def _():
        sent = []
        U, L = Plane(sent), Ring(sent, 0)
        U.forward(0)
        U.spread(1, -1)
        L.step(1)
        U.hop2()
        own_small()
        L.step(2)
        U.forward(1, -1)
        U.spread(2, -2)
        U.hop3()
        U.forward(2, -2)
        L.last()
        got("sib", lo.at[lslot(0, 1)], 1)
        U.spread(3, -3)
        U.spread(4)
        for b in range(4):
            lower_factors(0, b)
        U.forward(3, -3, 4)
        U.end(0, 1, -1, 2, -2, 3, -3)
        for b in range(4):
            upper_factors(0, b)
        base()
        lower_ready(1)
        got("masks", xmasks)
        for b in range(4):
            lower_factors(1, b)
        U.end(4)
        for copy in sent:
            copy.wait_send()

    @pl.when(core == 1)
    def _():
        sent = []
        U, L = Plane(sent), Ring(sent, 1)
        U.forward(0)
        U.spread(1, -1)
        U.hop2()
        own_small()
        L.cross()
        U.forward(1, -1)
        U.spread(2, -2)
        U.hop3()
        L.step(1)
        U.forward(2, -2)
        got("sib", lo.at[lslot(0, 0)], 0)
        U.spread(3, -3)
        U.spread(4)
        L.step(2)
        lower_ready(0)
        for b in range(4):
            lower_factors(0, b)
        U.forward(3, -3, 4)
        L.last()
        U.end(0, 1, -1, 2, -2, 3, -3)
        for b in range(4):
            upper_factors(0, b)
        base()
        got("masks", xmasks)
        for b in range(4):
            lower_factors(1, b)
        U.end(4)
        for copy in sent:
            copy.wait_send()

    for b in range(4):
        upper_factors(1, b)
    fetch.wait()
    finish()

    for copy in begun:
        copy.wait_send()
    pltpu.make_async_copy(out_v, out_ref, local.at[1]).wait()


def on_device(trail, lower, upper, li, ui, above, left, order, rmask, cmask):
    operands = (lower[0], upper[0], li[0], ui[0], above[0], left[0], order[0], rmask[0], cmask[0])
    hbm = pl.BlockSpec(memory_space=pltpu.HBM)
    out = pl.pallas_call(
        kernel,
        out_shape=jax.ShapeDtypeStruct((W, W), BF16),
        in_specs=[hbm] * 10,
        out_specs=pl.BlockSpec(memory_space=pl.ANY),
        scratch_shapes=[pltpu.VMEM(a.shape, a.dtype) for a in operands]
        + [
            pltpu.VMEM((NB, PANEL), BF16),
            pltpu.VMEM((NB, CROSS), BF16),
            pltpu.VMEM((SUB, CROSS), BF16),
            pltpu.VMEM((2, SUB, PANEL), BF16),
            pltpu.VMEM((2, 2 * NB, PANEL), BF16),
            pltpu.VMEM((4, NB, NB), BF16),
            pltpu.VMEM((8, 128), F32),
            pltpu.VMEM((8, 128), F32),
            pltpu.VMEM((2, W, 2 * NB), BF16),
            pltpu.VMEM((2, 2 * NB, W), BF16),
            pltpu.VMEM((W, W), F32),
            pltpu.VMEM((W, W), BF16),
            pltpu.VMEM((W, W), BF16),
            pltpu.SemaphoreType.DMA((COPIES,)),
            pltpu.SemaphoreType.DMA((COPIES,)),
            pltpu.SemaphoreType.DMA((11,)),
        ],
        compiler_params=pltpu.CompilerParams(
            collective_id=0, has_side_effects=True, vmem_limit_bytes=60 * 2**20
        ),
        name="panels_update",
    )(trail[:, 0, :], *operands)
    return out[:, None, :]


def solution(mesh):
    placed = (
        P("row", "layer", "col"),
        P("layer", None, "col", "row"),
        P("layer", None, "row", None, "col"),
        P("layer", None, None, None),
        P("layer", None, None, None),
        P("layer", None, None),
        P("layer", None, None),
        P("layer", None, None),
        P("layer", None, "row"),
        P("layer", None, None, "col"),
    )
    return jax.shard_map(
        on_device, mesh=mesh, in_specs=placed, out_specs=P("row", "layer", "col"), check_vma=False
    )
```
